128 devices in a mesh: dp: 8 (over x, core), ctx: 16 (over y, z).
Axes of the slice: x: 4, y: 4, z: 4, core: 2. Of those that a mesh axis runs over, the one named last changes fastest.
Arguments:
- queries: bfloat16 [8, 2048, 4096], P('dp', 'ctx'), may hold values from -8 to 8
- keys: bfloat16 [8, 2048, 512], P('dp', 'ctx'), may hold values from -8 to 8
- values: bfloat16 [8, 2048, 512], P('dp', 'ctx'), may hold values from -6 to 6
- cotangent: bfloat16 [8, 2048, 4096], P('dp', 'ctx'), may hold values from -6 to 6
- out_weight: bfloat16 [4096, 4096], P('ctx'), may hold values from -0.09375 to 0.09375
- doc_lengths: int32 [8, 8], P('dp'), may hold values from 1 to 1024, as said below
Outputs:
- query_grad: bfloat16 [8, 2048, 4096], P('dp', 'ctx')
- key_grad: bfloat16 [8, 2048, 512], P('dp', 'ctx')
- value_grad: bfloat16 [8, 2048, 512], P('dp', 'ctx')
- weight_grad: bfloat16 [4096, 4096], P('ctx', 'dp')
The draws below stay inside these ranges and needn't reach their ends.
Inputs may be any that keep to these rules, and one draw needn't show every extreme that they name: `doc_lengths`: in every sequence the lengths sum to 2048 and one document has exactly 1024 positions.
All inputs are finite; a program needn't handle non-finite values.
Results may differ from the reference program's by a relative error of at most 0.0085.
The reference program's roundings to bfloat16 on the way count: a program that leaves them out, or rounds other values in their place, can miss the bound.
Values may be sent and summed in bfloat16 or wider, within the bound.
No kernel may reach another device: no remote copies, remote signals or barrier semaphores. Data moves between devices by JAX's collectives and lax.ppermute only.
A program may use at most 192 MiB of HBM per device.

```python
from functools import partial
import jax
import jax.numpy as jnp
from jax import lax

QUERY_HEAD_COUNT = 32
KEY_VALUE_HEADS = 4
HEAD_SIZE = 128
OUT = 4096
DOCS = 8
SEQUENCE_LENGTH = 2048
SEQUENCE_COUNT = 8
MOSTDOC = 1024


def make_docs(key):
    lengths_key = jax.random.fold_in(key, 101)

    def one_sequence(seq_key):
        big_index = jax.random.randint(jax.random.fold_in(seq_key, 1), (), 0, DOCS)
        small_weights = jax.random.randint(jax.random.fold_in(seq_key, 2), (DOCS - 1,), 1, 8)
        remainder = SEQUENCE_LENGTH - MOSTDOC
        shares = 1 + (remainder - (DOCS - 1)) * small_weights // jnp.sum(small_weights)
        shares = shares.at[0].add(remainder - jnp.sum(shares))
        doc_slots = jnp.arange(DOCS, dtype=jnp.int32)
        source = jnp.clip(doc_slots - (doc_slots > big_index).astype(jnp.int32), 0, DOCS - 2)
        lengths_row = jnp.where(doc_slots == big_index, MOSTDOC, shares[source]).astype(jnp.int32)
        big_start = jnp.sum(jnp.where(doc_slots < big_index, lengths_row, 0)).astype(jnp.int32)
        return (lengths_row, big_start)
    seq_keys = jax.random.split(lengths_key, SEQUENCE_COUNT)
    lengths, starts = jax.vmap(one_sequence)(seq_keys)
    return lengths


def draw_doc_lengths(key, part):
    lengths = make_docs(key)
    return lengths


def draw_queries(key, part):
    key = jax.random.fold_in(key, 7)
    sampled_draws = jnp.clip(jax.random.normal(key, (SEQUENCE_COUNT, SEQUENCE_LENGTH, QUERY_HEAD_COUNT, HEAD_SIZE), jnp.float32), -8.0, 8.0)
    return sampled_draws.reshape(SEQUENCE_COUNT, SEQUENCE_LENGTH, QUERY_HEAD_COUNT * HEAD_SIZE).astype(jnp.bfloat16)


def draw_keys(key, part):
    key = jax.random.fold_in(key, 8)
    sampled_draws = jnp.clip(jax.random.normal(key, (SEQUENCE_COUNT, SEQUENCE_LENGTH, KEY_VALUE_HEADS, HEAD_SIZE), jnp.float32), -8.0, 8.0)
    return sampled_draws.reshape(SEQUENCE_COUNT, SEQUENCE_LENGTH, KEY_VALUE_HEADS * HEAD_SIZE).astype(jnp.bfloat16)


def strengthened(entries, key, source, target, parts, factor):
    def block_of(position):
        return (jnp.arange(entries.shape[position]) // (entries.shape[position] // parts)).reshape((-1,) + (1,) * (entries.ndim - 1 - position))

    one_side = jax.random.permutation(key, parts)[block_of(target)]
    second = (block_of(target) + parts // 2) % parts
    return jnp.where((block_of(source) == one_side) | (block_of(source) == second), factor * entries, entries)


def block_levels(key, dims, shards, low, top_value):
    def one(position, parts):
        draws = jax.random.uniform(jax.random.fold_in(jax.random.fold_in(key, 6), position), (parts,), jnp.float32, low / len(shards), top_value / len(shards))
        return jnp.repeat(jnp.exp(draws), dims[position] // parts).reshape((-1,) + (1,) * (len(dims) - position - 1))

    factor_of = one(*shards[0])
    for cut in shards[1:]:
        factor_of = factor_of * one(*cut)
    return factor_of


def gaussian(rng, shape, spread, limit, cuts=(), held_as=jnp.bfloat16):
    values = spread * jax.random.normal(rng, shape, jnp.float32)
    if cuts:
        values = values * block_levels(rng, shape, cuts, -0.22, 0.18)
    return jnp.clip(values, -limit, limit).astype(held_as)


def noise_with(key, extent, spread, reach, cuts, heavy, held_as=jnp.bfloat16):
    drawn = spread * jax.random.normal(key, extent, jnp.float32)
    if cuts:
        drawn = drawn * block_levels(key, extent, cuts, -0.22, 0.18)
    return jnp.clip(strengthened(drawn, jax.random.fold_in(key, 3), *heavy), -reach, reach).astype(held_as)


def setup_inputs(seed: int = 0) -> dict:
    arg_keys = jax.random.split(jax.random.key(seed), 7)
    return {
        "queries": draw_queries(jax.random.fold_in(arg_keys[6], 71), 0),
        "keys": draw_keys(jax.random.fold_in(arg_keys[6], 71), 0),
        "values": gaussian(arg_keys[2], (SEQUENCE_COUNT, SEQUENCE_LENGTH, KEY_VALUE_HEADS * HEAD_SIZE), 1.0, 6.0, ((0, 8), (1, 16))),
        "cotangent": noise_with(arg_keys[3], (SEQUENCE_COUNT, SEQUENCE_LENGTH, OUT), 1.0, 6.0, ((0, 8), (1, 16)), (0, 2, 8, 2.0)),
        "out_weight": gaussian(arg_keys[4], (QUERY_HEAD_COUNT * HEAD_SIZE, OUT), (QUERY_HEAD_COUNT * HEAD_SIZE) ** -0.5, 0.09375, ((0, 16),)),
        "doc_lengths": draw_doc_lengths(jax.random.fold_in(arg_keys[6], 71), 0),
    }


MASKED = -1.0e30


def documents_of(lengths_row):
    segment_ends = jnp.cumsum(lengths_row)
    positions = jnp.arange(SEQUENCE_LENGTH, dtype=jnp.int32)
    return jnp.sum((segment_ends[None, :] <= positions[:, None]).astype(jnp.int32), axis=1)


def one_head(query_head, key_head, value_head, grad_head, allowed):
    scaling = HEAD_SIZE ** -0.5
    scores = jnp.dot(query_head, key_head.T, preferred_element_type=jnp.float32) * scaling
    scores = jnp.where(allowed, scores, MASKED)
    row_max = jnp.max(scores, axis=1, keepdims=True)
    weights = jnp.where(allowed, jnp.exp(scores - row_max), 0.0)
    probabilities = (weights / jnp.sum(weights, axis=1, keepdims=True)).astype(jnp.bfloat16)
    attended = jnp.dot(probabilities, value_head, preferred_element_type=jnp.float32).astype(jnp.bfloat16)
    row_dot = jnp.sum(grad_head.astype(jnp.float32) * attended.astype(jnp.float32), axis=1, keepdims=True)
    prob_grad = jnp.dot(grad_head, value_head.T, preferred_element_type=jnp.float32)
    score_grad = (probabilities.astype(jnp.float32) * (prob_grad - row_dot)).astype(jnp.bfloat16)
    query_part = (jnp.dot(score_grad, key_head, preferred_element_type=jnp.float32) * scaling).astype(jnp.bfloat16)
    key_portion = jnp.dot(score_grad.T, query_head, preferred_element_type=jnp.float32) * scaling
    value_portion = jnp.dot(probabilities.T, grad_head, preferred_element_type=jnp.float32)
    return attended, query_part, key_portion, value_portion


def one_sequence(out_weight, inputs):
    query_seq, key_sequence, value_sequence, grad_seq, lengths_row = inputs
    group_width = QUERY_HEAD_COUNT // KEY_VALUE_HEADS
    documents = documents_of(lengths_row)
    positions = jnp.arange(SEQUENCE_LENGTH, dtype=jnp.int32)
    allowed = (positions[None, :] <= positions[:, None]) & (documents[None, :] == documents[:, None])
    grad_out = jnp.dot(grad_seq, out_weight.T, preferred_element_type=jnp.float32).astype(jnp.bfloat16)
    query_split = query_seq.reshape(SEQUENCE_LENGTH, QUERY_HEAD_COUNT, HEAD_SIZE).transpose(1, 0, 2)
    key_pieces_split = jnp.repeat(key_sequence.reshape(SEQUENCE_LENGTH, KEY_VALUE_HEADS, HEAD_SIZE).transpose(1, 0, 2), group_width, axis=0)
    value_pieces_split = jnp.repeat(value_sequence.reshape(SEQUENCE_LENGTH, KEY_VALUE_HEADS, HEAD_SIZE).transpose(1, 0, 2), group_width, axis=0)
    grad_split = grad_out.reshape(SEQUENCE_LENGTH, QUERY_HEAD_COUNT, HEAD_SIZE).transpose(1, 0, 2)

    def head_step(pieces):
        return one_head(pieces[0], pieces[1], pieces[2], pieces[3], allowed)

    attended, query_part, key_portion, value_portion = lax.map(head_step, (query_split, key_pieces_split, value_pieces_split, grad_split))
    key_total_sum = key_portion.reshape(KEY_VALUE_HEADS, group_width, SEQUENCE_LENGTH, HEAD_SIZE).sum(axis=1)
    value_total_sum = value_portion.reshape(KEY_VALUE_HEADS, group_width, SEQUENCE_LENGTH, HEAD_SIZE).sum(axis=1)
    attended_rows = attended.transpose(1, 0, 2).reshape(SEQUENCE_LENGTH, QUERY_HEAD_COUNT * HEAD_SIZE)
    query_rows = query_part.transpose(1, 0, 2).reshape(SEQUENCE_LENGTH, QUERY_HEAD_COUNT * HEAD_SIZE)
    key_row_block = key_total_sum.transpose(1, 0, 2).reshape(SEQUENCE_LENGTH, KEY_VALUE_HEADS * HEAD_SIZE).astype(jnp.bfloat16)
    value_row_block = value_total_sum.transpose(1, 0, 2).reshape(SEQUENCE_LENGTH, KEY_VALUE_HEADS * HEAD_SIZE).astype(jnp.bfloat16)
    return attended_rows, query_rows, key_row_block, value_row_block


def reference(queries, keys, values, cotangent, out_weight, doc_lengths):
    attended, query_grad, key_grad, value_grad = lax.map(partial(one_sequence, out_weight), (queries, keys, values, cotangent, doc_lengths))
    flat_attended = attended.reshape(SEQUENCE_COUNT * SEQUENCE_LENGTH, QUERY_HEAD_COUNT * HEAD_SIZE)
    flat_grad = cotangent.reshape(SEQUENCE_COUNT * SEQUENCE_LENGTH, OUT)
    weight_grad = jnp.dot(flat_attended.T, flat_grad, preferred_element_type=jnp.float32).astype(jnp.bfloat16)
    return query_grad, key_grad, value_grad, weight_grad
```

```python
import jax
import jax.numpy as jnp
from jax import lax
from jax.experimental import pallas as pl
from jax.experimental.pallas import tpu as pltpu
from jax.sharding import PartitionSpec as P

HEAD = 128
TILE = 256
LONGEST = 1024
SPAN = LONGEST // TILE + 1
MASKED = -1e30
SCALING = HEAD ** (-0.5)
F32 = jnp.float32
BF16 = jnp.bfloat16
NT = (((1,), (1,)), ((), ()))
TN = (((0,), (0,)), ((), ()))
NN = (((1,), (0,)), ((), ()))


def dot(a, b, dims):
    return lax.dot_general(a, b, dims, preferred_element_type=F32)


def document_starts(ends_ref, positions):
    start = jnp.zeros_like(positions)
    for d in range(ends_ref.shape[1]):
        end = ends_ref[0, d]
        start = jnp.maximum(start, jnp.where(end <= positions, end, 0))
    return start


def first_block(ends_ref, row):
    start = jnp.int32(0)
    for d in range(ends_ref.shape[1]):
        end = ends_ref[0, d]
        start = jnp.maximum(start, jnp.where(end <= row, end, 0))
    return start // TILE


def masked_scores(ends_ref, step, key_start, key_rows, query):
    count = key_rows.shape[0]
    rows = step * TILE + lax.broadcasted_iota(jnp.int32, (1, TILE), 1)
    starts = document_starts(ends_ref, rows)
    keys = key_start + lax.broadcasted_iota(jnp.int32, (count, TILE), 0)
    scores = dot(key_rows, query, NT) * SCALING
    return jnp.where((keys >= starts) & (keys <= rows), scores, MASKED)


def by_span(ends_ref, step, run):
    blocks = step - first_block(ends_ref, step * TILE) + 1
    for count in range(1, SPAN + 1):
        @pl.when(blocks == count)
        def _():
            run(count, pl.multiple_of((step - (count - 1)) * TILE, TILE))


def forward_kernel(ends_ref, query_ref, kv_ref, attended_ref, stats_ref, value_t):
    step = pl.program_id(0)

    @pl.when(step == 0)
    def _():
        value_t[...] = kv_ref[:, HEAD:].T
        stats_ref[...] = jnp.zeros_like(stats_ref)

    def run(count, key_start):
        span = pl.ds(key_start, count * TILE)
        key_rows = kv_ref[span, :HEAD]
        for h in range(2):
            cols = slice(h * HEAD, (h + 1) * HEAD)
            scores = masked_scores(ends_ref, step, key_start, key_rows, query_ref[:, cols])
            top = jnp.max(scores, axis=0, keepdims=True)
            weights = jnp.exp(scores - top)
            inverse = 1.0 / jnp.sum(weights, axis=0, keepdims=True)
            probs = (weights * inverse).astype(BF16)
            attended_t = dot(value_t[:, span], probs, NN)
            attended_ref[:, cols] = attended_t.T.astype(BF16)
            stats_ref[h : h + 1, :] = top
            stats_ref[2 + h : 3 + h, :] = inverse

    by_span(ends_ref, step, run)


def attention_forward(ends, qkv):
    tokens = qkv.shape[0]
    return pl.pallas_call(
        forward_kernel,
        grid=(tokens // TILE,),
        in_specs=[
            pl.BlockSpec(memory_space=pltpu.SMEM),
            pl.BlockSpec((TILE, 2 * HEAD), lambda i: (i, 0)),
            pl.BlockSpec((tokens, 2 * HEAD), lambda i: (0, 1)),
        ],
        out_specs=[
            pl.BlockSpec((TILE, 2 * HEAD), lambda i: (i, 0)),
            pl.BlockSpec((8, TILE), lambda i: (0, i)),
        ],
        out_shape=[
            jax.ShapeDtypeStruct((tokens, 2 * HEAD), BF16),
            jax.ShapeDtypeStruct((8, tokens), F32),
        ],
        scratch_shapes=[pltpu.VMEM((HEAD, tokens), BF16)],
        compiler_params=pltpu.CompilerParams(vmem_limit_bytes=40 * 2**20),
        cost_estimate=pl.CostEstimate(flops=1500000000, bytes_accessed=4 * 2**20, transcendentals=3000000),
        name="attention_forward",
    )(ends, qkv, qkv)


def backward_kernel(ends_ref, query_ref, kv_ref, grad_ref, attended_ref, stats_ref, out_ref, key_t, key_sum, value_sum):
    step = pl.program_id(0)

    @pl.when(step == 0)
    def _():
        key_t[...] = kv_ref[:, :HEAD].T
        key_sum[...] = jnp.zeros_like(key_sum)
        value_sum[...] = jnp.zeros_like(value_sum)

    row_start = pl.multiple_of(step * TILE, TILE)

    def run(count, key_start):
        span = pl.ds(key_start, count * TILE)
        key_rows = kv_ref[span, :HEAD]
        value_rows = kv_ref[span, HEAD:]
        key_part = jnp.zeros((count * TILE, HEAD), F32)
        value_part = jnp.zeros((count * TILE, HEAD), F32)
        for h in range(2):
            cols = slice(h * HEAD, (h + 1) * HEAD)
            query = query_ref[:, cols]
            grad = grad_ref[:, cols]
            products = grad.astype(F32) * attended_ref[:, cols].astype(F32)
            row_dot = jnp.sum(products.T, axis=0, keepdims=True)
            scores = masked_scores(ends_ref, step, key_start, key_rows, query)
            probs = (jnp.exp(scores - stats_ref[h : h + 1, :]) * stats_ref[2 + h : 3 + h, :]).astype(BF16)
            prob_grad = dot(value_rows, grad, NT)
            score_grad = (probs.astype(F32) * (prob_grad - row_dot)).astype(BF16)
            query_t = dot(key_t[:, span], score_grad, NN) * SCALING
            out_ref[pl.ds(row_start, TILE), cols] = query_t.T.astype(BF16)
            key_part += dot(score_grad, query, NN)
            value_part += dot(probs, grad, NN)
        key_sum[span, :] += key_part
        value_sum[span, :] += value_part

    by_span(ends_ref, step, run)

    @pl.when(step == pl.num_programs(0) - 1)
    def _():
        out_ref[:, 2 * HEAD : 3 * HEAD] = (key_sum[...] * SCALING).astype(BF16)
        out_ref[:, 3 * HEAD :] = value_sum[...].astype(BF16)


def attention_backward(ends, qkv, grad_out, attended, stats):
    tokens = qkv.shape[0]
    return pl.pallas_call(
        backward_kernel,
        grid=(tokens // TILE,),
        in_specs=[
            pl.BlockSpec(memory_space=pltpu.SMEM),
            pl.BlockSpec((TILE, 2 * HEAD), lambda i: (i, 0)),
            pl.BlockSpec((tokens, 2 * HEAD), lambda i: (0, 1)),
            pl.BlockSpec((TILE, 2 * HEAD), lambda i: (i, 0)),
            pl.BlockSpec((TILE, 2 * HEAD), lambda i: (i, 0)),
            pl.BlockSpec((8, TILE), lambda i: (0, i)),
        ],
        out_specs=pl.BlockSpec((tokens, 4 * HEAD), lambda i: (0, 0)),
        out_shape=jax.ShapeDtypeStruct((tokens, 4 * HEAD), BF16),
        scratch_shapes=[
            pltpu.VMEM((HEAD, tokens), BF16),
            pltpu.VMEM((tokens, HEAD), F32),
            pltpu.VMEM((tokens, HEAD), F32),
        ],
        compiler_params=pltpu.CompilerParams(vmem_limit_bytes=48 * 2**20),
        cost_estimate=pl.CostEstimate(flops=4000000000, bytes_accessed=6 * 2**20, transcendentals=3000000),
        name="attention_backward",
    )(ends, qkv, qkv, grad_out, attended, stats)


def weight_kernel(rows, attended_ref, *refs):
    out_ref = refs[-1]
    total = jnp.zeros(out_ref.shape, F32)
    start = 0
    for count, ref in zip(rows, refs[:-1]):
        total += dot(attended_ref[:, start : start + count], ref[...], NN)
        start += count
    out_ref[...] = total.astype(BF16)


def weight_terms(attended_t, chunks):
    features, tokens = attended_t.shape
    out = chunks[0].shape[1]
    width = 512
    rows = tuple(c.shape[0] for c in chunks)

    def kernel(*refs):
        weight_kernel(rows, *refs)

    return pl.pallas_call(
        kernel,
        grid=(out // width,),
        in_specs=[pl.BlockSpec((features, tokens), lambda i: (0, 0))]
        + [pl.BlockSpec((r, width), lambda i: (0, i)) for r in rows],
        out_specs=pl.BlockSpec((features, width), lambda i: (0, i)),
        out_shape=jax.ShapeDtypeStruct((features, out), BF16),
        compiler_params=pltpu.CompilerParams(vmem_limit_bytes=40 * 2**20),
        cost_estimate=pl.CostEstimate(
            flops=2 * features * tokens * out, bytes_accessed=2 * tokens * out, transcendentals=0
        ),
        name="weight_terms",
    )(attended_t, *chunks)


def body(queries, keys, values, cotangent, out_weight, doc_lengths):
    tokens = queries.shape[1]
    ctx = lax.axis_index("ctx")
    y, z = ctx // 4, ctx % 4
    x = lax.axis_index("dp") // 2
    core = lax.axis_index("dp") % 2

    along_z = lambda a, s: lax.ppermute(a, "ctx", [(4 * i + j, 4 * i + (j + s) % 4) for i in range(4) for j in range(4)])
    along_y = lambda a, s: lax.ppermute(a, "ctx", [(4 * i + j, 4 * ((i + s) % 4) + j) for i in range(4) for j in range(4)])
    along_x = lambda a, s: lax.ppermute(a, "dp", [(2 * i + j, 2 * ((i + s) % 4) + j) for i in range(4) for j in range(2)])
    other_core = lambda a: lax.ppermute(a, "dp", [(i, i ^ 1) for i in range(8)])

    grad_rows = cotangent[0]
    half = tokens // 2
    out = grad_rows.shape[1]

    query_parts = queries[0].reshape(tokens, 16, 2 * HEAD).transpose(1, 0, 2)
    key_parts = jnp.repeat(keys[0].reshape(tokens, 4, HEAD).transpose(1, 0, 2), 4, axis=0)
    value_parts = jnp.repeat(values[0].reshape(tokens, 4, HEAD).transpose(1, 0, 2), 4, axis=0)
    qkv = lax.all_to_all(
        jnp.concatenate([query_parts, key_parts, value_parts], axis=2), "ctx", split_axis=0, concat_axis=0, tiled=True
    ).reshape(16 * tokens, 4 * HEAD)
    ends = jnp.cumsum(doc_lengths, axis=1).astype(jnp.int32)

    def ring(block, shift, own):
        plus, minus = shift(block, 1), shift(block, -1)
        middle = block.shape[0] // 2
        far_top, far_bottom = shift(plus[:middle], 1), shift(minus[middle:], -1)
        return (own, block), ((own + 3) % 4, plus), ((own + 1) % 4, minus), ((own + 2) % 4, far_top, far_bottom)

    def collect(block, shift, own):
        (p0, b0), (p1, b1), (p2, b2), (p3, t3, u3) = ring(block, shift, own)
        rows = block.shape[0]
        buffer = jnp.zeros((4 * rows, out), BF16)
        for start, part in (
            (p0 * rows, b0),
            (p1 * rows, b1),
            (p2 * rows, b2),
            (p3 * rows, t3),
            (p3 * rows + rows // 2, u3),
        ):
            buffer = lax.dynamic_update_slice(buffer, part, (start, 0))
        return buffer

    upper = collect(grad_rows[:half], along_z, z)
    lower = collect(grad_rows[half:], along_y, y)
    upper_ring = ring(upper, along_y, y)
    lower_ring = ring(lower, along_z, z)

    attended, stats = attention_forward(ends, qkv)

    attended_grid = attended.reshape(4, 4, 2, half, 2 * HEAD)
    grad_out = jnp.zeros((4, 4, 2, half, 2 * HEAD), BF16)
    chunks, attended_parts = [], []
    for kind, entries in ((0, upper_ring), (1, lower_ring)):
        for position, *arrays in entries:
            for piece, array in enumerate(arrays):
                groups = array.shape[0] // half
                first = piece * groups
                if kind == 0:
                    start = (position, first, 0, 0, 0)
                    sizes = (1, groups, 1, half, 2 * HEAD)
                else:
                    start = (first, position, 1, 0, 0)
                    sizes = (groups, 1, 1, half, 2 * HEAD)
                rows = dot(array, out_weight, NT).astype(BF16)
                grad_out = lax.dynamic_update_slice(grad_out, rows.reshape(sizes), start)
                attended_parts.append(lax.dynamic_slice(attended_grid, start, sizes).reshape(groups * half, 2 * HEAD))
                chunks.append(array)
    grad_out = grad_out.reshape(16 * tokens, 2 * HEAD)
    attended_t = jnp.concatenate(attended_parts, axis=0).T

    partial = weight_terms(attended_t, chunks)
    features = partial.shape[0]
    by_device = partial.reshape(features, 4, 2, out // 8)
    kept = lax.dynamic_index_in_dim(by_device, core, 2, False)
    sent = lax.dynamic_index_in_dim(by_device, 1 - core, 2, False)
    chip = (kept.astype(F32) + other_core(sent).astype(F32)).astype(BF16).transpose(1, 0, 2)
    pieces = [lax.dynamic_index_in_dim(chip, (x + s) % 4, 0, False) for s in range(4)]
    weight_sum = pieces[0].astype(F32)
    for s in (1, 3, 2):
        weight_sum = weight_sum + along_x(pieces[s], s).astype(F32)
    weight_grad = weight_sum.astype(BF16)

    grads = attention_backward(ends, qkv, grad_out, attended, stats)
    back = lax.all_to_all(grads.reshape(16, tokens, 4 * HEAD), "ctx", split_axis=0, concat_axis=0, tiled=True)
    query_grad = back[:, :, : 2 * HEAD].transpose(1, 0, 2).reshape(1, tokens, 32 * HEAD)

    def shared(part):
        total = part.astype(F32).reshape(4, 4, tokens, HEAD).sum(axis=1)
        return total.astype(BF16).transpose(1, 0, 2).reshape(1, tokens, 4 * HEAD)

    key_grad = shared(back[:, :, 2 * HEAD : 3 * HEAD])
    value_grad = shared(back[:, :, 3 * HEAD :])
    return query_grad, key_grad, value_grad, weight_grad


def solution(mesh):
    return jax.shard_map(
        body,
        mesh=mesh,
        in_specs=(
            P("dp", "ctx", None),
            P("dp", "ctx", None),
            P("dp", "ctx", None),
            P("dp", "ctx", None),
            P("ctx", None),
            P("dp", None),
        ),
        out_specs=(
            P("dp", "ctx", None),
            P("dp", "ctx", None),
            P("dp", "ctx", None),
            P("ctx", "dp"),
        ),
        check_vma=False,
    )
```
